1024 devices in a mesh: ctx: 128 (over z, y, core), head: 8 (over x).
Axes of the slice: x: 8, y: 8, z: 8, core: 2. Of those that a mesh axis runs over, the one named last changes fastest.
Arguments:
- keys: bfloat16 [8, 32768, 512], P('head', 'ctx'), may hold values from -24 to 24
- values: bfloat16 [8, 32768, 512], P('head', 'ctx'), may hold values from -6 to 6
- queries: bfloat16 [8, 32768, 512], P('head', 'ctx'), may hold values from -6 to 6
- token_lr: float32 [8, 32768], P('head', 'ctx'), may hold values from 0.005 to 0.05
- w_gate: bfloat16 [8, 512, 512], P('head'), may hold values from -0.25 to 0.25
- w_up: bfloat16 [8, 512, 512], P('head'), may hold values from -0.25 to 0.25
- w_down: bfloat16 [8, 512, 512], P('head'), may hold values from -0.25 to 0.25
- mom_gate: float32 [8, 512, 512], P('head', 'ctx'), may hold values from -6 to 6
- mom_up: float32 [8, 512, 512], P('head', 'ctx'), may hold values from -6 to 6
Outputs:
- applied: bfloat16 [8, 32768, 512], P('head', 'ctx')
- new_mom_gate: float32 [8, 512, 512], P('head', 'ctx')
- new_mom_up: float32 [8, 512, 512], P('head', 'ctx')
The draws below stay inside these ranges and needn't reach their ends.
All inputs are finite; a program needn't handle non-finite values.
Results may differ from the reference program's by a relative error of at most 0.008.
Values may be sent and summed in bfloat16 or wider, within the bound.
A program may use at most 32 MiB of HBM per device.

```python
import math
import jax
import jax.numpy as jnp
from jax import lax

DH = 512
FH = 512
HEADS = 8
TOKENS = 32768


def raised(array, stream_key, source, target, parts, factor):
    owner, partner = [(jnp.arange(array.shape[position]) // (array.shape[position] // parts)).reshape([-1 if axis == position else 1 for axis in range(array.ndim)]) for position in (source, target)]
    chosen = jax.random.permutation(stream_key, parts)[partner]
    strong = (owner == chosen) | (owner == (partner + parts // 2) % parts)
    return jnp.where(strong, factor * array, array)


def level_of(own_key, extent, split, low, top_value):
    loudness, own = 1.0, jax.random.fold_in(own_key, 6)
    for axis_at, parts in split:
        draws = jnp.exp(jax.random.uniform(jax.random.fold_in(own, axis_at), (parts,), jnp.float32, low / len(split), top_value / len(split)))
        loudness = loudness * jnp.repeat(draws, extent[axis_at] // parts).reshape([-1 if axis == axis_at else 1 for axis in range(len(extent))])
    return loudness


def scatter_about(rng, dims, spread, reach, cuts=(), held_as=jnp.bfloat16):
    result = jax.random.normal(rng, dims, jnp.float32) * spread
    if len(cuts) > 0:
        result = level_of(rng, dims, cuts, -0.22, 0.18) * result
    return jnp.clip(result, min=-reach, max=reach).astype(held_as)


def bell_draw_with(rng, dims, spread, bound, cuts, heavy, dtype=jnp.bfloat16):
    array = spread * jax.random.normal(rng, dims, jnp.float32)
    if cuts:
        array = array * level_of(rng, dims, cuts, -0.22, 0.18)
    return jnp.clip(raised(array, jax.random.fold_in(rng, 3), *heavy), -bound, bound).astype(dtype)


def setup_inputs(seed: int = 0) -> dict:
    key_list = jax.random.split(jax.random.key(seed), 10)
    return {
        "keys": bell_draw_with(key_list[0], (HEADS, TOKENS, DH), 1.0, 24.0, ((0, 8), (1, 128)), (1, 2, 128, 5.5)),
        "values": scatter_about(key_list[1], (HEADS, TOKENS, DH), 1.0, 6.0, ((0, 8), (1, 128))),
        "queries": scatter_about(key_list[2], (HEADS, TOKENS, DH), 1.0, 6.0, ((0, 8), (1, 128))),
        "token_lr": jnp.clip(jnp.exp(math.log(0.05) - 2.3025851 * jax.random.uniform(key_list[3], (HEADS, TOKENS), jnp.float32) ** level_of(key_list[3], (HEADS, TOKENS), ((0, 8), (1, 128)), -0.2, 0.2)), 0.005, 0.05),
        "w_gate": scatter_about(key_list[4], (HEADS, DH, FH), DH ** -0.5, 0.25, ((0, 8),)),
        "w_up": scatter_about(key_list[5], (HEADS, DH, FH), DH ** -0.5, 0.25, ((0, 8),)),
        "w_down": scatter_about(key_list[6], (HEADS, FH, DH), FH ** -0.5, 0.25, ((0, 8),)),
        "mom_gate": scatter_about(key_list[7], (HEADS, DH, FH), 1.0, 6.0, ((0, 8), (1, 128)), jnp.float32),
        "mom_up": scatter_about(key_list[8], (HEADS, DH, FH), 1.0, 6.0, ((0, 8), (1, 128)), jnp.float32),
    }


def one_head(args):
    keys, values, queries, token_lr, w_gate, w_up, w_down, mom_gate, mom_up = args
    pre_gate = jnp.dot(keys, w_gate, preferred_element_type=jnp.float32)
    pre_up = jnp.dot(keys, w_up, preferred_element_type=jnp.float32)
    dout = (-token_lr[:, None] * values.astype(jnp.float32)).astype(jnp.bfloat16)
    zgrad = jnp.dot(dout, w_down.T, preferred_element_type=jnp.float32)
    sig = jax.nn.sigmoid(pre_gate)
    grad_gate = (zgrad * pre_up * sig * (1.0 + pre_gate * (1.0 - sig))).astype(jnp.bfloat16)
    grad_up = (zgrad * pre_gate * sig).astype(jnp.bfloat16)
    g_gate = jnp.dot(keys.T, grad_gate, preferred_element_type=jnp.float32)
    g_up = jnp.dot(keys.T, grad_up, preferred_element_type=jnp.float32)
    new_gate = 0.9 * mom_gate + g_gate
    new_up = 0.9 * mom_up + g_up
    step_gate = new_gate / jnp.sqrt(lax.optimization_barrier(jnp.mean(new_gate * new_gate, axis=-1, keepdims=True)) + 1e-05)
    step_up = new_up / jnp.sqrt(lax.optimization_barrier(jnp.mean(new_up * new_up, axis=-1, keepdims=True)) + 1e-05)
    gate_next = (w_gate.astype(jnp.float32) - 0.02 * step_gate).astype(jnp.bfloat16)
    up_next = (w_up.astype(jnp.float32) - 0.02 * step_up).astype(jnp.bfloat16)
    q_gate = jnp.dot(queries, gate_next, preferred_element_type=jnp.float32)
    q_up = jnp.dot(queries, up_next, preferred_element_type=jnp.float32)
    hidden = (jax.nn.silu(q_gate) * q_up).astype(jnp.bfloat16)
    applied = jnp.dot(hidden, w_down, preferred_element_type=jnp.float32).astype(jnp.bfloat16)
    return (applied, new_gate, new_up)

def reference(keys, values, queries, token_lr, w_gate, w_up, w_down, mom_gate, mom_up):
    applied, new_gate, new_up = lax.map(one_head, (keys, values, queries, token_lr, w_gate, w_up, w_down, mom_gate, mom_up))
    return (applied, new_gate, new_up)
```

```python
import jax
import jax.numpy as jnp
from jax import lax
from jax.experimental import pallas as pl
from jax.experimental.pallas import tpu as pltpu
from jax.sharding import PartitionSpec as P

MESH = pl.DeviceIdType.MESH
F32, BF16 = jnp.float32, jnp.bfloat16
RING = 8
D = 512
T = 256
OFFSETS = (0, 1, -1, 2, -2, 3, -3, 4)


def dot(a, b):
    return jnp.dot(a, b, preferred_element_type=F32)


def dot_t(a, b):
    return lax.dot_general(a, b, (((1,), (1,)), ((), ())), preferred_element_type=F32)


def ring(v):
    return lax.rem(v + RING, RING)


def selector(z, y, matrix, sign, wide):
    rows = D * 2 if wide else D
    row = lax.broadcasted_iota(jnp.int32, (rows, 128), 0)
    lane = lax.broadcasted_iota(jnp.int32, (rows, 128), 1)
    low = 4 if wide else 3
    first, second = row >> (low + 3), (row >> low) & 7

    def place(origin, slot):
        off = jnp.where((slot & 1) == 1, (slot + 1) >> 1, -(slot >> 1))
        return (origin + sign * off + RING) & (RING - 1)

    if matrix == 0:
        chip = place(z, second) * RING + place(y, first)
    else:
        chip = place(z, first) * RING + place(y, second)
    feature = chip * 8 + (row & 7)
    if wide:
        feature = jnp.where((row & 8) == 0, feature, -1)
    parts = [
        jnp.where(feature == lane + 128 * k, 1.0, 0.0).astype(BF16) for k in range(D // 128)
    ]
    return jnp.concatenate(parts, axis=1)


def stack(block):
    return jnp.concatenate([block[:, : D // 2], block[:, D // 2 :]], axis=0)


def kernel(
    keys, values, queries, lr, w_gate, w_up, w_down, mom_gate, mom_up,
    out, out_gate, out_up,
    keys_v, values_v, queries_v, lr_v, w_v, down_v, mom_v, mom_in, mom_send, mom_recv,
    keys_t, grads, pair_send, pair_recv, hop_send, hop_recv, total, rows_send, rows_recv,
    weights, q_left, q_right,
    load_sem, pair_ss, pair_rs, hop_ss, hop_rs, row_ss, row_rs,
    near_ss, near_rs, far_ss, far_rs, fwd_ss, fwd_rs, mom_ss, mom_rs,
):
    me = lax.axis_index("ctx")
    c = lax.rem(me, 2)
    chip = lax.div(me, 2)
    y = lax.rem(chip, RING)
    z = lax.div(chip, RING)
    mine, other = c, 1 - c

    def device(zz, yy, cc):
        return {"ctx": (ring(zz) * RING + ring(yy)) * 2 + cc}

    partner = device(z, y, 1 - c)
    first = [device(z + c * o, y + (1 - c) * o, c) for o in OFFSETS]
    second = [device(z + (1 - c) * o, y + c * o, c) for o in OFFSETS]

    loads = [
        pltpu.make_async_copy(src, dst, load_sem.at[k])
        for k, (src, dst) in enumerate(
            (
                (keys.at[0], keys_v),
                (w_gate.at[0], w_v.at[0]),
                (w_up.at[0], w_v.at[1]),
                (lr, lr_v),
                (values.at[0], values_v),
                (w_down.at[0], down_v),
                (mom_gate.at[0], mom_v.at[0]),
                (mom_up.at[0], mom_v.at[1]),
                (queries.at[0], queries_v),
            )
        )
    ]
    for load in loads:
        load.start()

    barrier = pltpu.get_barrier_semaphore()
    for peer in [partner] + first[1:] + second[1:]:
        pl.semaphore_signal(barrier, inc=1, device_id=peer, device_id_type=MESH)

    def remote(src, dst, ss, rs, to):
        return pltpu.make_async_remote_copy(
            src_ref=src, dst_ref=dst, send_sem=ss, recv_sem=rs, device_id=to, device_id_type=MESH
        )

    pick = [selector(z, y, m, 1, False) for m in range(2)]
    loads[0].wait()
    for m in range(2):
        keys_t[m] = dot_t(pick[m], keys_v[...]).astype(BF16)
    for k in (1, 2, 3, 4, 5):
        loads[k].wait()
    rate = jnp.broadcast_to(lr_v[...], (128, T)).T
    rate = jnp.concatenate([rate] * (D // 128), axis=1)
    dout = (-rate * values_v[...].astype(F32)).astype(BF16)
    for h in range(2):
        cols = pl.ds(h * (D // 2), D // 2)
        gate = dot(keys_v[...], w_v[0, :, cols])
        up = dot(keys_v[...], w_v[1, :, cols])
        zgrad = dot_t(dout, down_v[cols, :])
        sig = jax.nn.sigmoid(gate)
        zs = zgrad * sig
        grads[0, :, cols] = (zs * up * (1.0 + gate * (1.0 - sig))).astype(BF16)
        grads[1, :, cols] = (zs * gate).astype(BF16)

    pl.semaphore_wait(barrier, 2 * RING - 1)

    groups = (3, 2, 1, 0)
    pairs = []
    for g in groups:
        rows = pl.ds(g * 128, 128)
        pair_send[rows, :] = dot(keys_t[other, rows, :], grads[other]).astype(BF16)
        copy = remote(pair_send.at[rows], pair_recv.at[rows], pair_ss.at[g], pair_rs.at[g], partner)
        copy.start()
        pairs.append(copy)
    loads[6].wait()
    loads[7].wait()
    mom_copy = remote(mom_v.at[other], mom_in, mom_ss.at[0], mom_rs.at[0], partner)
    mom_copy.start()

    hops = [None] * RING
    for copy, g in zip(pairs, groups):
        rows = pl.ds(g * 128, 128)
        part = dot(keys_t[mine, rows, :], grads[mine])
        copy.wait_recv()
        part = part + pair_recv[rows, :].astype(F32)
        for j in (2 * g + 1, 2 * g):
            half = part[64:] if j % 2 else part[:64]
            if j == 0:
                total[...] = half
            else:
                hop_send[j] = half.astype(BF16)
                hops[j] = remote(
                    hop_send.at[j], hop_recv.at[j], hop_ss.at[j], hop_rs.at[j], first[j]
                )
                hops[j].start()

    loads[8].wait()
    for m in range(2):
        left = dot_t(queries_v[...], selector(z, y, m, -1, True))
        q_left[m] = left.astype(BF16)
        q_right[m] = pltpu.roll(left, 8, 1).astype(BF16)
    pair_row = pl.multiple_of(lax.div(chip, 2) * 16, 16)
    w_rows = w_v[mine, pl.ds(pair_row, 16), :].astype(F32)
    w_rows = stack(jnp.where(lax.rem(chip, 2) == 0, w_rows[:8], w_rows[8:]))
    mom_copy.wait_recv()
    own, theirs = mom_v[mine], mom_in[...]
    even = c == 0
    momentum = stack(
        jnp.concatenate([jnp.where(even, own, theirs), jnp.where(even, theirs, own)], axis=0)
    )

    acc = total[...]
    for j in range(1, RING):
        hops[j].wait_recv()
        acc = acc + hop_recv[j].astype(F32)

    row_copies = [None] * RING
    for d in range(RING - 1, 0, -1):
        rows_send[d] = stack(acc[d * 8 : d * 8 + 8]).astype(BF16)
        row_copies[d] = remote(
            rows_send.at[d], rows_recv.at[d], row_ss.at[d], row_rs.at[d], second[d]
        )
        row_copies[d].start()
    grad = stack(acc[:8])
    for d in range(1, RING):
        row_copies[d].wait_recv()
        grad = grad + rows_recv[d].astype(F32)
    fresh = 0.9 * momentum + grad
    square = jnp.sum(fresh * fresh, axis=1, keepdims=True)
    square = (square[:8] + square[8:]) * (1.0 / D)
    scale = 1.0 / jnp.sqrt(jnp.concatenate([square, square], axis=0) + 1e-05)
    weights[mine, pl.ds(0, 16), :] = (w_rows - 0.02 * (fresh * scale)).astype(BF16)

    near = [None] * RING
    for d in range(RING - 1, 0, -1):
        near[d] = remote(
            weights.at[mine, pl.ds(0, 16)],
            weights.at[mine, pl.ds(16 * d, 16)],
            near_ss.at[d], near_rs.at[d], second[d],
        )
        near[d].start()
    whole = jnp.concatenate([fresh[:8], fresh[8:]], axis=1)
    keep = jnp.where(even, whole[:4], whole[4:])
    mom_send[...] = jnp.where(even, whole[4:], whole[:4])
    mom_back = remote(mom_send, mom_recv, mom_ss.at[1], mom_rs.at[1], partner)
    mom_back.start()
    for d in range(1, RING):
        near[d].wait_recv()

    far = [None] * RING
    block = lambda j: weights.at[mine, pl.ds(128 * j, 128)]
    for j in range(RING - 1, 0, -1):
        far[j] = remote(block(0), block(j), far_ss.at[j], far_rs.at[j], first[j])
        far[j].start()
    forward = []
    for j in range(RING):
        if j:
            far[j].wait_recv()
        copy = remote(block(j), block(j), fwd_ss.at[j], fwd_rs.at[j], partner)
        copy.start()
        forward.append(copy)
    mom_back.wait_recv()
    back = mom_recv[...]
    out_gate[0] = jnp.where(even, keep, back)
    out_up[0] = jnp.where(even, back, keep)
    for copy in forward:
        copy.wait_recv()

    for h in range(2):
        cols = pl.ds(h * (D // 2), D // 2)
        q = q_left if h == 0 else q_right
        gate = dot(q[0], weights[0])
        up = dot(q[1], weights[1])
        grads[0, :, cols] = (gate * jax.nn.sigmoid(gate) * up).astype(BF16)
    out[0] = dot(grads[0], down_v[...]).astype(BF16)

    for copy in pairs + hops[1:] + row_copies[1:] + near[1:] + far[1:] + forward + [mom_copy, mom_back]:
        copy.wait_send()


def per_device(*args):
    hbm = pl.BlockSpec(memory_space=pltpu.HBM)
    vmem = pl.BlockSpec(memory_space=pltpu.VMEM)
    dma = pltpu.SemaphoreType.DMA
    return pl.pallas_call(
        kernel,
        out_shape=(
            jax.ShapeDtypeStruct((1, T, D), BF16),
            jax.ShapeDtypeStruct((1, 4, D), F32),
            jax.ShapeDtypeStruct((1, 4, D), F32),
        ),
        in_specs=[hbm] * 9,
        out_specs=(vmem, vmem, vmem),
        scratch_shapes=[
            pltpu.VMEM((T, D), BF16),
            pltpu.VMEM((T, D), BF16),
            pltpu.VMEM((T, D), BF16),
            pltpu.VMEM((1, T), F32),
            pltpu.VMEM((2, D, D), BF16),
            pltpu.VMEM((D, D), BF16),
            pltpu.VMEM((2, 4, D), F32),
            pltpu.VMEM((4, D), F32),
            pltpu.VMEM((4, D), F32),
            pltpu.VMEM((4, D), F32),
            pltpu.VMEM((2, D, T), BF16),
            pltpu.VMEM((2, T, D), BF16),
            pltpu.VMEM((D, D), BF16),
            pltpu.VMEM((D, D), BF16),
            pltpu.VMEM((RING, 64, D), BF16),
            pltpu.VMEM((RING, 64, D), BF16),
            pltpu.VMEM((64, D), F32),
            pltpu.VMEM((RING, 16, D // 2), BF16),
            pltpu.VMEM((RING, 16, D // 2), BF16),
            pltpu.VMEM((2, 2 * D, D // 2), BF16),
            pltpu.VMEM((2, T, 2 * D), BF16),
            pltpu.VMEM((2, T, 2 * D), BF16),
            dma((9,)),
            dma((4,)), dma((4,)),
            dma((RING,)), dma((RING,)),
            dma((RING,)), dma((RING,)),
            dma((RING,)), dma((RING,)),
            dma((RING,)), dma((RING,)),
            dma((RING,)), dma((RING,)),
            dma((2,)), dma((2,)),
        ],
        compiler_params=pltpu.CompilerParams(
            collective_id=0, has_side_effects=True, vmem_limit_bytes=63_000_000
        ),
        cost_estimate=pl.CostEstimate(
            flops=16 * T * D * D, bytes_accessed=3 * 1024 * 1024, transcendentals=2 * T * D
        ),
        name="update_and_apply",
    )(*args)


def solution(mesh):
    tokens = P("head", "ctx", None)
    weight = P("head", None, None)
    return jax.shard_map(
        per_device,
        mesh=mesh,
        in_specs=(tokens, tokens, tokens, P("head", "ctx"), weight, weight, weight, tokens, tokens),
        out_specs=(tokens, tokens, tokens),
        check_vma=False,
    )
```

```python
import jax
import jax.numpy as jnp
from jax import lax
from jax.experimental import pallas as pl
from jax.experimental.pallas import tpu as pltpu
from jax.sharding import PartitionSpec as P

MESH = pl.DeviceIdType.MESH
F32, BF16 = jnp.float32, jnp.bfloat16
RING = 8
D = 512
T = 256
Y_ORDER = (1, 0, 2, 3, 7, 6, 4, 5)
Z_ORDER = (0, 1, 2, 3, 4, 5, 6, 7)
NEAR_FIRST = (1, 7, 2, 6, 3, 5, 4)


def dot(a, b):
    return jnp.dot(a, b, preferred_element_type=F32)


def dot_t(a, b):
    return lax.dot_general(a, b, (((1,), (1,)), ((), ())), preferred_element_type=F32)


def one_hot(picked, width):
    lane = lax.broadcasted_iota(jnp.int32, picked.shape, 1)
    parts = [
        jnp.where(picked == lane + 128 * k, 1.0, 0.0).astype(BF16) for k in range(width // 128)
    ]
    return jnp.concatenate(parts, axis=1)


def swapped(row):
    return ((row >> 3) & 7) * 64 + (row >> 6) * 8 + (row & 7)


def kernel(
    keys, values, queries, lr, w_gate, w_up, w_down, mom_gate, mom_up,
    out, out_gate, out_up,
    keys_v, values_v, queries_v, lr_v, w_v, down_v, mom_v, mom_in, mom_send, mom_recv,
    keys_t, grads, pair_send, pair_recv, hop_send, hop_recv, total, part_send, part_recv,
    weights, queries_p,
    load_sem, pair_ss, pair_rs, hop_ss, hop_rs, part_ss, part_rs,
    far_ss, far_rs, fwd_ss, fwd_rs, mom_ss, mom_rs,
):
    me = lax.axis_index("ctx")
    c = lax.rem(me, 2)
    chip = lax.div(me, 2)
    y = lax.rem(chip, RING)
    z = lax.div(chip, RING)
    mine, other = c, 1 - c
    even = c == 0
    at1 = jnp.where(even, y, z)
    at2 = jnp.where(even, z, y)
    partner = {"ctx": me + 1 - 2 * c}

    def first(s):
        return {"ctx": jnp.where(even, z * RING + s, s * RING + y) * 2 + c}

    def second(s):
        return {"ctx": jnp.where(even, s * RING + y, z * RING + s) * 2 + c}

    def beside(at, k):
        return (at + k) & (RING - 1)

    loads = [
        pltpu.make_async_copy(src, dst, load_sem.at[k])
        for k, (src, dst) in enumerate(
            (
                (keys.at[0], keys_v),
                (w_gate.at[0], w_v.at[0]),
                (w_up.at[0], w_v.at[1]),
                (lr, lr_v),
                (values.at[0], values_v),
                (w_down.at[0], down_v),
                (mom_gate.at[0], mom_v.at[0]),
                (mom_up.at[0], mom_v.at[1]),
                (queries.at[0], queries_v),
            )
        )
    ]
    for load in loads:
        load.start()

    barrier = pltpu.get_barrier_semaphore()
    for peer in (
        [partner]
        + [first(beside(at1, k)) for k in range(1, RING)]
        + [second(beside(at2, k)) for k in range(1, RING)]
    ):
        pl.semaphore_signal(barrier, inc=1, device_id=peer, device_id_type=MESH)

    def remote(src, dst, ss, rs, to):
        return pltpu.make_async_remote_copy(
            src_ref=src, dst_ref=dst, send_sem=ss, recv_sem=rs, device_id=to, device_id_type=MESH
        )

    eye = one_hot(lax.broadcasted_iota(jnp.int32, (D, 128), 0), D)
    loads[0].wait()
    turned = dot_t(eye, keys_v[...])
    keys_t[1] = turned.astype(BF16)
    keys_t[0] = jnp.concatenate(
        [turned[64 * b + 8 * a : 64 * b + 8 * a + 8] for a in range(RING) for b in range(RING)], axis=0
    ).astype(BF16)
    for k in (1, 2, 3, 4, 5):
        loads[k].wait()
    rate = jnp.broadcast_to(lr_v[...], (128, T)).T
    rate = jnp.concatenate([rate] * (D // 128), axis=1)
    dout = (-rate * values_v[...].astype(F32)).astype(BF16)
    for h in range(2):
        cols = pl.ds(h * (D // 2), D // 2)
        gate = dot(keys_v[...], w_v[0, :, cols])
        up = dot(keys_v[...], w_v[1, :, cols])
        zgrad = dot_t(dout, down_v[cols, :])
        sig = jax.nn.sigmoid(gate)
        zs = zgrad * sig
        grads[0, :, cols] = (zs * up * (1.0 + gate * (1.0 - sig))).astype(BF16)
        grads[1, :, cols] = (zs * gate).astype(BF16)

    pl.semaphore_wait(barrier, 2 * RING - 1)

    turns = (2, 1, 3, 0)
    theirs = jnp.where(even, z, y) >> 1
    pairs = []
    for t in turns:
        g = (theirs + t) & 3
        rows = pl.ds(pl.multiple_of(g * 128, 128), 128)
        pair_send[rows, :] = dot(keys_t[other, rows, :], grads[other]).astype(BF16)
        copy = remote(pair_send.at[rows], pair_recv.at[rows], pair_ss.at[t], pair_rs.at[t], partner)
        copy.start()
        pairs.append(copy)
    loads[6].wait()
    loads[7].wait()
    mom_copy = remote(mom_v.at[other], mom_in, mom_ss.at[0], mom_rs.at[0], partner)
    mom_copy.start()

    def hop(s):
        return remote(hop_send.at[s], hop_recv.at[at1], hop_ss.at[s], hop_rs.at[at1], first(s))

    for copy, t in zip(pairs, turns):
        g = ((at1 >> 1) + t) & 3
        rows = pl.ds(pl.multiple_of(g * 128, 128), 128)
        part = dot(keys_t[mine, rows, :], grads[mine])
        copy.wait_recv()
        part = part + pair_recv[rows, :].astype(F32)
        if t:
            for half in range(2):
                s = 2 * g + half
                hop_send[s] = part[64 * half : 64 * half + 64].astype(BF16)
                hop(s).start()
        else:
            low = (at1 & 1) == 0
            total[...] = jnp.where(low, part[:64], part[64:])
            s = at1 + 1 - 2 * (at1 & 1)
            hop_send[s] = jnp.where(low, part[64:], part[:64]).astype(BF16)
            hop(s).start()

    loads[8].wait()
    order = one_hot(swapped(lax.broadcasted_iota(jnp.int32, (D, 128), 0)), D)
    queries_p[...] = dot_t(queries_v[...], order).astype(BF16)
    row = lax.broadcasted_iota(jnp.int32, (64, 128), 0)
    feature = jnp.where(even, (row >> 3) * 64 + at1 * 8 + (row & 7), at1 * 64 + row)
    w_rows = dot(one_hot(feature, D), w_v[mine])
    mom_copy.wait_recv()
    own, given = mom_v[mine], mom_in[...]
    here = pl.ds(pl.multiple_of(at2 * 8, 8), 8)
    momentum = jnp.concatenate([jnp.where(even, own, given), jnp.where(even, given, own)], axis=0)
    total[here, :] = total[here, :] + 0.9 * momentum

    acc = total[...]
    for k in NEAR_FIRST:
        s = beside(at1, k)
        remote(hop_send.at[s], hop_recv.at[s], hop_ss.at[s], hop_rs.at[s], first(s)).wait_recv()
        acc = acc + hop_recv[s].astype(F32)
    part_send[...] = acc.astype(BF16)

    def share(s):
        return remote(part_send, part_recv.at[at2], part_ss.at[s], part_rs.at[at2], second(s))

    for sy, sz in zip(Y_ORDER, Z_ORDER):
        s = jnp.where(even, sz, sy)

        @pl.when(s != at2)
        def _(s=s):
            share(s).start()

    for k in NEAR_FIRST:
        s = beside(at2, k)
        remote(part_send, part_recv.at[s], part_ss.at[s], part_rs.at[s], second(s)).wait_recv()
        acc = acc + part_recv[s].astype(F32)
    scale = 0.02 / jnp.sqrt(jnp.mean(acc * acc, axis=1, keepdims=True) + 1e-05)

    def block(s):
        return weights.at[mine, pl.ds(pl.multiple_of(s * 64, 64), 64)]

    block(at1)[...] = (w_rows - acc * scale).astype(BF16)

    def spread(s):
        return remote(block(at1), block(at1), far_ss.at[s], far_rs.at[at1], first(s))

    def forward(s):
        return remote(block(s), block(s), fwd_ss.at[s], fwd_rs.at[s], partner)

    for sy, sz in zip(Y_ORDER, Z_ORDER):
        s = jnp.where(even, sy, sz)

        @pl.when(s != at1)
        def _(s=s):
            spread(s).start()

    forward(at1).start()
    total[...] = acc
    fresh = total[here, :]
    keep = jnp.where(even, fresh[:4], fresh[4:])
    mom_send[...] = jnp.where(even, fresh[4:], fresh[:4])
    mom_back = remote(mom_send, mom_recv, mom_ss.at[1], mom_rs.at[1], partner)
    mom_back.start()
    for k in NEAR_FIRST:
        s = beside(at1, k)
        remote(block(s), block(s), far_ss.at[s], far_rs.at[s], first(s)).wait_recv()
        forward(s).start()
    mom_back.wait_recv()
    back = mom_recv[...]
    out_gate[0] = jnp.where(even, keep, back)
    out_up[0] = jnp.where(even, back, keep)
    for s in range(RING):
        theirs_s = weights.at[other, pl.ds(64 * s, 64)]
        remote(theirs_s, theirs_s, fwd_ss.at[s], fwd_rs.at[s], partner).wait_recv()

    for h in range(2):
        cols = pl.ds(h * (D // 2), D // 2)
        gate = dot(queries_p[...], weights[0, :, cols])
        up = dot(queries_v[...], weights[1, :, cols])
        grads[0, :, cols] = (gate * jax.nn.sigmoid(gate) * up).astype(BF16)
    out[0] = dot(grads[0], down_v[...]).astype(BF16)

    for k in range(1, RING):
        hop(beside(at1, k)).wait_send()
        share(beside(at2, k)).wait_send()
        spread(beside(at1, k)).wait_send()
    for s in range(RING):
        forward(s).wait_send()
    for copy in pairs + [mom_copy, mom_back]:
        copy.wait_send()


def store_kernel(a, b, c, a_out, b_out, c_out, sem):
    copies = [
        pltpu.make_async_copy(src, dst, sem.at[k])
        for k, (src, dst) in enumerate(((a, a_out), (b, b_out), (c, c_out)))
    ]
    for copy in copies:
        copy.start()
    for copy in copies:
        copy.wait()


def per_device(*args):
    hbm = pl.BlockSpec(memory_space=pl.ANY)
    vmem = pl.BlockSpec(memory_space=pltpu.VMEM)
    dma = pltpu.SemaphoreType.DMA
    shapes = (
        jax.ShapeDtypeStruct((1, T, D), BF16),
        jax.ShapeDtypeStruct((1, 4, D), F32),
        jax.ShapeDtypeStruct((1, 4, D), F32),
    )
    results = pl.pallas_call(
        kernel,
        out_shape=tuple(pltpu.VMEM(s.shape, s.dtype) for s in shapes),
        in_specs=[hbm] * 9,
        out_specs=(vmem, vmem, vmem),
        scratch_shapes=[
            pltpu.VMEM((T, D), BF16),
            pltpu.VMEM((T, D), BF16),
            pltpu.VMEM((T, D), BF16),
            pltpu.VMEM((1, T), F32),
            pltpu.VMEM((2, D, D), BF16),
            pltpu.VMEM((D, D), BF16),
            pltpu.VMEM((2, 4, D), F32),
            pltpu.VMEM((4, D), F32),
            pltpu.VMEM((4, D), F32),
            pltpu.VMEM((4, D), F32),
            pltpu.VMEM((2, D, T), BF16),
            pltpu.VMEM((2, T, D), BF16),
            pltpu.VMEM((D, D), BF16),
            pltpu.VMEM((D, D), BF16),
            pltpu.VMEM((RING, 64, D), BF16),
            pltpu.VMEM((RING, 64, D), BF16),
            pltpu.VMEM((64, D), F32),
            pltpu.VMEM((64, D), BF16),
            pltpu.VMEM((RING, 64, D), BF16),
            pltpu.VMEM((2, D, D), BF16),
            pltpu.VMEM((T, D), BF16),
            dma((9,)),
            dma((4,)), dma((4,)),
            dma((RING,)), dma((RING,)),
            dma((RING,)), dma((RING,)),
            dma((RING,)), dma((RING,)),
            dma((RING,)), dma((RING,)),
            dma((2,)), dma((2,)),
        ],
        compiler_params=pltpu.CompilerParams(
            collective_id=0, has_side_effects=True, vmem_limit_bytes=63_000_000
        ),
        cost_estimate=pl.CostEstimate(
            flops=16 * T * D * D, bytes_accessed=3 * 1024 * 1024, transcendentals=2 * T * D
        ),
        name="update_and_apply",
    )(*args)
    return pl.pallas_call(
        store_kernel,
        out_shape=shapes,
        in_specs=[hbm] * 3,
        out_specs=(hbm, hbm, hbm),
        scratch_shapes=[dma((3,))],
        compiler_params=pltpu.CompilerParams(vmem_limit_bytes=1024 * 1024),
        name="store",
    )(*results)


def solution(mesh):
    tokens = P("head", "ctx", None)
    weight = P("head", None, None)
    return jax.shard_map(
        per_device,
        mesh=mesh,
        in_specs=(tokens, tokens, tokens, P("head", "ctx"), weight, weight, weight, tokens, tokens),
        out_specs=(tokens, tokens, tokens),
        check_vma=False,
    )
```

```python
import jax
import jax.numpy as jnp
from jax import lax
from jax.experimental import pallas as pl
from jax.experimental.pallas import tpu as pltpu
from jax.sharding import PartitionSpec as P

MESH = pl.DeviceIdType.MESH
F32, BF16 = jnp.float32, jnp.bfloat16
RING = 8
D = 512
T = 256
PARTS = 2
PART = 64 // PARTS
Y_ORDER = (0, 1, 2, 3, 7, 6, 4, 5)
Z_ORDER = (0, 1, 2, 3, 4, 5, 6, 7)
NEAR_FIRST = (1, 7, 2, 6, 3, 5, 4)


def dot(a, b):
    return jnp.dot(a, b, preferred_element_type=F32)


def dot_t(a, b):
    return lax.dot_general(a, b, (((1,), (1,)), ((), ())), preferred_element_type=F32)


def one_hot(picked, width):
    lane = lax.broadcasted_iota(jnp.int32, picked.shape, 1)
    parts = [
        jnp.where(picked == lane + 128 * k, 1.0, 0.0).astype(BF16) for k in range(width // 128)
    ]
    return jnp.concatenate(parts, axis=1)


def swapped(row):
    return ((row >> 3) & 7) * 64 + (row >> 6) * 8 + (row & 7)


def kernel(
    keys, values, queries, lr, w_gate, w_up, w_down, mom_gate, mom_up,
    out, out_gate, out_up,
    keys_v, values_v, queries_v, lr_v, w_v, down_v, mom_v, mom_in, mom_send, mom_recv,
    keys_t, grads, pair_send, pair_recv, hop_send, hop_recv, total, part_send, part_recv,
    weights, queries_p,
    load_sem, pair_ss, pair_rs, hop_ss, hop_rs, part_ss, part_rs,
    far_ss, far_rs, fwd_ss, fwd_rs, mom_ss, mom_rs,
):
    me = lax.axis_index("ctx")
    c = lax.rem(me, 2)
    chip = lax.div(me, 2)
    y = lax.rem(chip, RING)
    z = lax.div(chip, RING)
    mine, other = c, 1 - c
    even = c == 0
    at1 = jnp.where(even, y, z)
    at2 = jnp.where(even, z, y)
    partner = {"ctx": me + 1 - 2 * c}

    def first(s):
        return {"ctx": jnp.where(even, z * RING + s, s * RING + y) * 2 + c}

    def second(s):
        return {"ctx": jnp.where(even, s * RING + y, z * RING + s) * 2 + c}

    def beside(at, k):
        return (at + k) & (RING - 1)

    loads = [
        pltpu.make_async_copy(src, dst, load_sem.at[k])
        for k, (src, dst) in enumerate(
            (
                (keys.at[0], keys_v),
                (w_gate.at[0], w_v.at[0]),
                (w_up.at[0], w_v.at[1]),
                (lr, lr_v),
                (values.at[0], values_v),
                (w_down.at[0], down_v),
                (mom_gate.at[0], mom_v.at[0]),
                (mom_up.at[0], mom_v.at[1]),
                (queries.at[0], queries_v),
            )
        )
    ]
    for load in loads:
        load.start()

    barrier = pltpu.get_barrier_semaphore()
    for peer in (
        [partner]
        + [first(beside(at1, k)) for k in range(1, RING)]
        + [second(beside(at2, k)) for k in range(1, RING)]
    ):
        pl.semaphore_signal(barrier, inc=1, device_id=peer, device_id_type=MESH)

    def remote(src, dst, ss, rs, to):
        return pltpu.make_async_remote_copy(
            src_ref=src, dst_ref=dst, send_sem=ss, recv_sem=rs, device_id=to, device_id_type=MESH
        )

    eye = one_hot(lax.broadcasted_iota(jnp.int32, (D, 128), 0), D)
    loads[0].wait()
    turned = dot_t(eye, keys_v[...])
    keys_t[1] = turned.astype(BF16)
    keys_t[0] = jnp.concatenate(
        [turned[64 * b + 8 * a : 64 * b + 8 * a + 8] for a in range(RING) for b in range(RING)], axis=0
    ).astype(BF16)
    for k in (1, 2, 3, 4, 5):
        loads[k].wait()
    rate = jnp.broadcast_to(lr_v[...], (128, T)).T
    rate = jnp.concatenate([rate] * (D // 128), axis=1)
    dout = (-rate * values_v[...].astype(F32)).astype(BF16)
    for h in range(2):
        cols = pl.ds(h * (D // 2), D // 2)
        gate = dot(keys_v[...], w_v[0, :, cols])
        up = dot(keys_v[...], w_v[1, :, cols])
        zgrad = dot_t(dout, down_v[cols, :])
        sig = jax.nn.sigmoid(gate)
        zs = zgrad * sig
        grads[0, :, cols] = (zs * up * (1.0 + gate * (1.0 - sig))).astype(BF16)
        grads[1, :, cols] = (zs * gate).astype(BF16)

    pl.semaphore_wait(barrier, 2 * RING - 1)

    turns = (2, 1, 3, 0)
    theirs = jnp.where(even, z, y) >> 1
    pairs = []
    for t in turns:
        g = (theirs + t) & 3
        rows = pl.ds(pl.multiple_of(g * 128, 128), 128)
        pair_send[rows, :] = dot(keys_t[other, rows, :], grads[other]).astype(BF16)
        copy = remote(pair_send.at[rows], pair_recv.at[rows], pair_ss.at[t], pair_rs.at[t], partner)
        copy.start()
        pairs.append(copy)
    loads[6].wait()
    loads[7].wait()
    mom_copy = remote(mom_v.at[other], mom_in, mom_ss.at[0], mom_rs.at[0], partner)
    mom_copy.start()

    def span(h):
        return pl.ds(h * PART, PART)

    def hop(s, h, slot=None):
        slot = at1 if slot is None else slot
        return remote(
            hop_send.at[s, span(h)], hop_recv.at[slot, span(h)], hop_ss.at[s, h], hop_rs.at[slot, h], first(s)
        )

    sent = []
    for copy, t in zip(pairs, turns):
        g = ((at1 >> 1) + t) & 3
        rows = pl.ds(pl.multiple_of(g * 128, 128), 128)
        part = dot(keys_t[mine, rows, :], grads[mine])
        copy.wait_recv()
        part = part + pair_recv[rows, :].astype(F32)
        if t:
            for half in range(2):
                s = 2 * g + half
                hop_send[s] = part[64 * half : 64 * half + 64].astype(BF16)
                hop(s, 0).start()
                sent.append(s)
        else:
            low = (at1 & 1) == 0
            total[...] = jnp.where(low, part[:64], part[64:])
            s = at1 + 1 - 2 * (at1 & 1)
            hop_send[s] = jnp.where(low, part[64:], part[:64]).astype(BF16)
            hop(s, 0).start()
            sent.append(s)
    for h in range(1, PARTS):
        for s in sent:
            hop(s, h).start()

    loads[8].wait()
    order = one_hot(swapped(lax.broadcasted_iota(jnp.int32, (D, 128), 0)), D)
    queries_p[...] = dot_t(queries_v[...], order).astype(BF16)
    row = lax.broadcasted_iota(jnp.int32, (64, 128), 0)
    feature = jnp.where(even, (row >> 3) * 64 + at1 * 8 + (row & 7), at1 * 64 + row)
    w_rows = dot(one_hot(feature, D), w_v[mine])
    mom_copy.wait_recv()
    own, given = mom_v[mine], mom_in[...]
    here = pl.ds(pl.multiple_of(at2 * 8, 8), 8)
    momentum = jnp.concatenate([jnp.where(even, own, given), jnp.where(even, given, own)], axis=0)
    total[here, :] = total[here, :] + 0.9 * momentum

    def share(s, h, slot=None):
        slot = at2 if slot is None else slot
        return remote(
            part_send.at[span(h)], part_recv.at[slot, span(h)], part_ss.at[s, h], part_rs.at[slot, h], second(s)
        )

    sums = []
    for h in range(PARTS):
        acc = total[span(h), :]
        for k in NEAR_FIRST:
            s = beside(at1, k)
            hop(s, h, s).wait_recv()
            acc = acc + hop_recv[s, span(h), :].astype(F32)
        sums.append(acc)
        part_send[span(h), :] = acc.astype(BF16)
        for sy, sz in zip(Y_ORDER, Z_ORDER):
            s = jnp.where(even, sz, sy)

            @pl.when(s != at2)
            def _(s=s):
                share(s, h).start()

    def block(matrix, s, h):
        return weights.at[matrix, pl.ds(pl.multiple_of(s * 64 + h * PART, PART), PART)]

    def spread(s, h, slot=None):
        slot = at1 if slot is None else slot
        rows = block(mine, slot, h)
        return remote(rows, rows, far_ss.at[s, h], far_rs.at[slot, h], first(s))

    def forward(s, h):
        return remote(block(mine, s, h), block(mine, s, h), fwd_ss.at[s, h], fwd_rs.at[s, h], partner)

    for h in range(PARTS):
        acc = sums[h]
        for k in NEAR_FIRST:
            s = beside(at2, k)
            share(s, h, s).wait_recv()
            acc = acc + part_recv[s, span(h), :].astype(F32)
        total[span(h), :] = acc
        scale = 0.02 / jnp.sqrt(jnp.mean(acc * acc, axis=1, keepdims=True) + 1e-05)
        block(mine, at1, h)[...] = (w_rows[h * PART : h * PART + PART] - acc * scale).astype(BF16)
        for sy, sz in zip(Y_ORDER, Z_ORDER):
            s = jnp.where(even, sy, sz)

            @pl.when(s != at1)
            def _(s=s):
                spread(s, h).start()

        forward(at1, h).start()
    fresh = total[here, :]
    keep = jnp.where(even, fresh[:4], fresh[4:])
    mom_send[...] = jnp.where(even, fresh[4:], fresh[:4])
    mom_back = remote(mom_send, mom_recv, mom_ss.at[1], mom_rs.at[1], partner)
    mom_back.start()
    for h in range(PARTS):
        for k in NEAR_FIRST:
            s = beside(at1, k)
            spread(s, h, s).wait_recv()
            forward(s, h).start()
    mom_back.wait_recv()
    back = mom_recv[...]
    out_gate[0] = jnp.where(even, keep, back)
    out_up[0] = jnp.where(even, back, keep)
    for h in range(PARTS):
        for s in range(RING):
            rows = block(other, s, h)
            remote(rows, rows, fwd_ss.at[s, h], fwd_rs.at[s, h], partner).wait_recv()

    for h in range(2):
        cols = pl.ds(h * (D // 2), D // 2)
        gate = dot(queries_p[...], weights[0, :, cols])
        up = dot(queries_v[...], weights[1, :, cols])
        grads[0, :, cols] = (gate * jax.nn.sigmoid(gate) * up).astype(BF16)
    out[0] = dot(grads[0], down_v[...]).astype(BF16)

    for h in range(PARTS):
        for k in range(1, RING):
            hop(beside(at1, k), h).wait_send()
            share(beside(at2, k), h).wait_send()
            spread(beside(at1, k), h).wait_send()
        for s in range(RING):
            forward(s, h).wait_send()
    for copy in pairs + [mom_copy, mom_back]:
        copy.wait_send()


def store_kernel(a, b, c, a_out, b_out, c_out, sem):
    copies = [
        pltpu.make_async_copy(src, dst, sem.at[k])
        for k, (src, dst) in enumerate(((a, a_out), (b, b_out), (c, c_out)))
    ]
    for copy in copies:
        copy.start()
    for copy in copies:
        copy.wait()


def per_device(*args):
    hbm = pl.BlockSpec(memory_space=pl.ANY)
    vmem = pl.BlockSpec(memory_space=pltpu.VMEM)
    dma = pltpu.SemaphoreType.DMA
    shapes = (
        jax.ShapeDtypeStruct((1, T, D), BF16),
        jax.ShapeDtypeStruct((1, 4, D), F32),
        jax.ShapeDtypeStruct((1, 4, D), F32),
    )
    results = pl.pallas_call(
        kernel,
        out_shape=tuple(pltpu.VMEM(s.shape, s.dtype) for s in shapes),
        in_specs=[hbm] * 9,
        out_specs=(vmem, vmem, vmem),
        scratch_shapes=[
            pltpu.VMEM((T, D), BF16),
            pltpu.VMEM((T, D), BF16),
            pltpu.VMEM((T, D), BF16),
            pltpu.VMEM((1, T), F32),
            pltpu.VMEM((2, D, D), BF16),
            pltpu.VMEM((D, D), BF16),
            pltpu.VMEM((2, 4, D), F32),
            pltpu.VMEM((4, D), F32),
            pltpu.VMEM((4, D), F32),
            pltpu.VMEM((4, D), F32),
            pltpu.VMEM((2, D, T), BF16),
            pltpu.VMEM((2, T, D), BF16),
            pltpu.VMEM((D, D), BF16),
            pltpu.VMEM((D, D), BF16),
            pltpu.VMEM((RING, 64, D), BF16),
            pltpu.VMEM((RING, 64, D), BF16),
            pltpu.VMEM((64, D), F32),
            pltpu.VMEM((64, D), BF16),
            pltpu.VMEM((RING, 64, D), BF16),
            pltpu.VMEM((2, D, D), BF16),
            pltpu.VMEM((T, D), BF16),
            dma((9,)),
            dma((4,)), dma((4,)),
            dma((RING, PARTS)), dma((RING, PARTS)),
            dma((RING, PARTS)), dma((RING, PARTS)),
            dma((RING, PARTS)), dma((RING, PARTS)),
            dma((RING, PARTS)), dma((RING, PARTS)),
            dma((2,)), dma((2,)),
        ],
        compiler_params=pltpu.CompilerParams(
            collective_id=0, has_side_effects=True, vmem_limit_bytes=63_000_000
        ),
        cost_estimate=pl.CostEstimate(
            flops=16 * T * D * D, bytes_accessed=3 * 1024 * 1024, transcendentals=2 * T * D
        ),
        name="update_and_apply",
    )(*args)
    return pl.pallas_call(
        store_kernel,
        out_shape=shapes,
        in_specs=[hbm] * 3,
        out_specs=(hbm, hbm, hbm),
        scratch_shapes=[dma((3,))],
        compiler_params=pltpu.CompilerParams(vmem_limit_bytes=1024 * 1024),
        name="store",
    )(*results)


def solution(mesh):
    tokens = P("head", "ctx", None)
    weight = P("head", None, None)
    return jax.shard_map(
        per_device,
        mesh=mesh,
        in_specs=(tokens, tokens, tokens, P("head", "ctx"), weight, weight, weight, tokens, tokens),
        out_specs=(tokens, tokens, tokens),
        check_vma=False,
    )
```

```python
import jax
import jax.numpy as jnp
from jax import lax
from jax.experimental import pallas as pl
from jax.experimental.pallas import tpu as pltpu
from jax.sharding import PartitionSpec as P

MESH = pl.DeviceIdType.MESH
F32, BF16 = jnp.float32, jnp.bfloat16
RING = 8
D = 512
T = 256
PARTS = 2
PART = 64 // PARTS
Y_ORDER = (0, 1, 2, 3, 7, 6, 4, 5)
Z_ORDER = (0, 1, 2, 3, 4, 5, 6, 7)
NEAR_FIRST = (1, 7, 2, 6, 3, 5, 4)


def dot(a, b):
    return jnp.dot(a, b, preferred_element_type=F32)


def dot_t(a, b):
    return lax.dot_general(a, b, (((1,), (1,)), ((), ())), preferred_element_type=F32)


def one_hot(picked, width):
    lane = lax.broadcasted_iota(jnp.int32, picked.shape, 1)
    parts = [
        jnp.where(picked == lane + 128 * k, 1.0, 0.0).astype(BF16) for k in range(width // 128)
    ]
    return jnp.concatenate(parts, axis=1)


def swapped(row):
    return ((row >> 3) & 7) * 64 + (row >> 6) * 8 + (row & 7)


def kernel(
    keys, values, queries, lr, w_gate, w_up, w_down, mom_gate, mom_up,
    out, out_gate, out_up,
    keys_v, values_v, queries_v, lr_v, w_v, down_v, mom_v, mom_in, mom_send, mom_recv,
    keys_t, grads, pair_send, pair_recv, hop_send, hop_recv, total, part_send, part_recv,
    weights, queries_p,
    load_sem, pair_ss, pair_rs, hop_ss, hop_rs, part_ss, part_rs,
    far_ss, far_rs, fwd_ss, fwd_rs, mom_ss, mom_rs,
):
    me = lax.axis_index("ctx")
    c = lax.rem(me, 2)
    chip = lax.div(me, 2)
    y = lax.rem(chip, RING)
    z = lax.div(chip, RING)
    mine, other = c, 1 - c
    even = c == 0
    at1 = jnp.where(even, y, z)
    at2 = jnp.where(even, z, y)
    partner = {"ctx": me + 1 - 2 * c}

    def first(s):
        return {"ctx": jnp.where(even, z * RING + s, s * RING + y) * 2 + c}

    def second(s):
        return {"ctx": jnp.where(even, s * RING + y, z * RING + s) * 2 + c}

    def beside(at, k):
        return (at + k) & (RING - 1)

    loads = [
        pltpu.make_async_copy(src, dst, load_sem.at[k])
        for k, (src, dst) in enumerate(
            (
                (keys.at[0], keys_v),
                (w_gate.at[0], w_v.at[0]),
                (w_up.at[0], w_v.at[1]),
                (lr, lr_v),
                (values.at[0], values_v),
                (w_down.at[0], down_v),
                (mom_gate.at[0], mom_v.at[0]),
                (mom_up.at[0], mom_v.at[1]),
                (queries.at[0], queries_v),
            )
        )
    ]
    for load in loads:
        load.start()

    barrier = pltpu.get_barrier_semaphore()
    for peer in (
        [partner]
        + [first(beside(at1, k)) for k in range(1, RING)]
        + [second(beside(at2, k)) for k in range(1, RING)]
    ):
        pl.semaphore_signal(barrier, inc=1, device_id=peer, device_id_type=MESH)

    def remote(src, dst, ss, rs, to):
        return pltpu.make_async_remote_copy(
            src_ref=src, dst_ref=dst, send_sem=ss, recv_sem=rs, device_id=to, device_id_type=MESH
        )

    eye = one_hot(lax.broadcasted_iota(jnp.int32, (D, 128), 0), D)
    loads[0].wait()
    turned = dot_t(eye, keys_v[...])
    keys_t[1] = turned.astype(BF16)
    keys_t[0] = jnp.concatenate(
        [turned[64 * b + 8 * a : 64 * b + 8 * a + 8] for a in range(RING) for b in range(RING)], axis=0
    ).astype(BF16)
    for k in (1, 2, 3, 4, 5):
        loads[k].wait()
    rate = jnp.broadcast_to(lr_v[...], (128, T)).T
    rate = jnp.concatenate([rate] * (D // 128), axis=1)
    dout = (-rate * values_v[...].astype(F32)).astype(BF16)
    for h in range(2):
        cols = pl.ds(h * (D // 2), D // 2)
        gate = dot(keys_v[...], w_v[0, :, cols])
        up = dot(keys_v[...], w_v[1, :, cols])
        zgrad = dot_t(dout, down_v[cols, :])
        sig = jax.nn.sigmoid(gate)
        zs = zgrad * sig
        grads[0, :, cols] = (zs * up * (1.0 + gate * (1.0 - sig))).astype(BF16)
        grads[1, :, cols] = (zs * gate).astype(BF16)

    turns = (2, 1, 3, 0)
    theirs = jnp.where(even, z, y) >> 1
    pairs = []
    for t in turns:
        g = (theirs + t) & 3
        rows = pl.ds(pl.multiple_of(g * 128, 128), 128)
        pair_send[rows, :] = dot(keys_t[other, rows, :], grads[other]).astype(BF16)
        pairs.append(remote(pair_send.at[rows], pair_recv.at[rows], pair_ss.at[t], pair_rs.at[t], partner))
    pl.semaphore_wait(barrier, 2 * RING - 1)
    for copy in pairs:
        copy.start()
    loads[6].wait()
    loads[7].wait()
    mom_copy = remote(mom_v.at[other], mom_in, mom_ss.at[0], mom_rs.at[0], partner)
    mom_copy.start()

    def span(h):
        return pl.ds(h * PART, PART)

    def hop(s, h, slot=None):
        slot = at1 if slot is None else slot
        return remote(
            hop_send.at[s, span(h)], hop_recv.at[slot, span(h)], hop_ss.at[s, h], hop_rs.at[slot, h], first(s)
        )

    sent = []
    for copy, t in zip(pairs, turns):
        g = ((at1 >> 1) + t) & 3
        rows = pl.ds(pl.multiple_of(g * 128, 128), 128)
        part = dot(keys_t[mine, rows, :], grads[mine])
        copy.wait_recv()
        part = part + pair_recv[rows, :].astype(F32)
        if t:
            for half in range(2):
                s = 2 * g + half
                hop_send[s] = part[64 * half : 64 * half + 64].astype(BF16)
                hop(s, 0).start()
                sent.append(s)
        else:
            low = (at1 & 1) == 0
            total[...] = jnp.where(low, part[:64], part[64:])
            s = at1 + 1 - 2 * (at1 & 1)
            hop_send[s] = jnp.where(low, part[64:], part[:64]).astype(BF16)
            hop(s, 0).start()
            sent.append(s)
    for h in range(1, PARTS):
        for s in sent:
            hop(s, h).start()

    loads[8].wait()
    order = one_hot(swapped(lax.broadcasted_iota(jnp.int32, (D, 128), 0)), D)
    queries_p[...] = dot_t(queries_v[...], order).astype(BF16)
    row = lax.broadcasted_iota(jnp.int32, (64, 128), 0)
    feature = jnp.where(even, (row >> 3) * 64 + at1 * 8 + (row & 7), at1 * 64 + row)
    w_rows = dot(one_hot(feature, D), w_v[mine])
    mom_copy.wait_recv()
    own, given = mom_v[mine], mom_in[...]
    here = pl.ds(pl.multiple_of(at2 * 8, 8), 8)
    momentum = jnp.concatenate([jnp.where(even, own, given), jnp.where(even, given, own)], axis=0)
    total[here, :] = total[here, :] + 0.9 * momentum

    def share(s, h, slot=None):
        slot = at2 if slot is None else slot
        return remote(
            part_send.at[span(h)], part_recv.at[slot, span(h)], part_ss.at[s, h], part_rs.at[slot, h], second(s)
        )

    sums = []
    for h in range(PARTS):
        acc = total[span(h), :]
        for k in NEAR_FIRST:
            s = beside(at1, k)
            hop(s, h, s).wait_recv()
            acc = acc + hop_recv[s, span(h), :].astype(F32)
        sums.append(acc)
        part_send[span(h), :] = acc.astype(BF16)
        for sy, sz in zip(Y_ORDER, Z_ORDER):
            s = jnp.where(even, sz, sy)

            @pl.when(s != at2)
            def _(s=s):
                share(s, h).start()

    def block(matrix, s, h):
        return weights.at[matrix, pl.ds(pl.multiple_of(s * 64 + h * PART, PART), PART)]

    def spread(s, h, slot=None):
        slot = at1 if slot is None else slot
        rows = block(mine, slot, h)
        return remote(rows, rows, far_ss.at[s, h], far_rs.at[slot, h], first(s))

    def forward(s, matrix=None):
        rows = weights.at[mine if matrix is None else matrix, pl.ds(pl.multiple_of(s * 64, 64), 64)]
        return remote(rows, rows, fwd_ss.at[s, 0], fwd_rs.at[s, 0], partner)

    for h in range(PARTS):
        acc = sums[h]
        for k in NEAR_FIRST:
            s = beside(at2, k)
            share(s, h, s).wait_recv()
            acc = acc + part_recv[s, span(h), :].astype(F32)
        total[span(h), :] = acc
        scale = 0.02 / jnp.sqrt(jnp.mean(acc * acc, axis=1, keepdims=True) + 1e-05)
        block(mine, at1, h)[...] = (w_rows[h * PART : h * PART + PART] - acc * scale).astype(BF16)
        for sy, sz in zip(Y_ORDER, Z_ORDER):
            s = jnp.where(even, sy, sz)

            @pl.when(s != at1)
            def _(s=s):
                spread(s, h).start()

    forward(at1).start()
    fresh = total[here, :]
    keep = jnp.where(even, fresh[:4], fresh[4:])
    mom_send[...] = jnp.where(even, fresh[4:], fresh[:4])
    mom_back = remote(mom_send, mom_recv, mom_ss.at[1], mom_rs.at[1], partner)
    mom_back.start()
    for h in range(PARTS):
        for k in range(1, RING):
            hop(beside(at1, k), h).wait_send()
            share(beside(at2, k), h).wait_send()
    for copy in pairs + [mom_copy]:
        copy.wait_send()
    for h in range(PARTS):
        for k in NEAR_FIRST:
            s = beside(at1, k)
            spread(s, h, s).wait_recv()
            if h == PARTS - 1:
                forward(s).start()
    for h in range(PARTS):
        for k in range(1, RING):
            spread(beside(at1, k), h).wait_send()
    mom_back.wait_recv()
    back = mom_recv[...]
    out_gate[0] = jnp.where(even, keep, back)
    out_up[0] = jnp.where(even, back, keep)
    for s in range(RING):
        forward(s, other).wait_recv()

    for h in range(2):
        cols = pl.ds(h * (D // 2), D // 2)
        gate = dot(queries_p[...], weights[0, :, cols])
        up = dot(queries_v[...], weights[1, :, cols])
        grads[0, :, cols] = (gate * jax.nn.sigmoid(gate) * up).astype(BF16)
    out[0] = dot(grads[0], down_v[...]).astype(BF16)

    for s in range(RING):
        forward(s).wait_send()
    mom_back.wait_send()


def store_kernel(a, b, c, a_out, b_out, c_out, sem):
    copies = [
        pltpu.make_async_copy(src, dst, sem.at[k])
        for k, (src, dst) in enumerate(((a, a_out), (b, b_out), (c, c_out)))
    ]
    for copy in copies:
        copy.start()
    for copy in copies:
        copy.wait()


def per_device(*args):
    hbm = pl.BlockSpec(memory_space=pl.ANY)
    vmem = pl.BlockSpec(memory_space=pltpu.VMEM)
    dma = pltpu.SemaphoreType.DMA
    shapes = (
        jax.ShapeDtypeStruct((1, T, D), BF16),
        jax.ShapeDtypeStruct((1, 4, D), F32),
        jax.ShapeDtypeStruct((1, 4, D), F32),
    )
    results = pl.pallas_call(
        kernel,
        out_shape=tuple(pltpu.VMEM(s.shape, s.dtype) for s in shapes),
        in_specs=[hbm] * 9,
        out_specs=(vmem, vmem, vmem),
        scratch_shapes=[
            pltpu.VMEM((T, D), BF16),
            pltpu.VMEM((T, D), BF16),
            pltpu.VMEM((T, D), BF16),
            pltpu.VMEM((1, T), F32),
            pltpu.VMEM((2, D, D), BF16),
            pltpu.VMEM((D, D), BF16),
            pltpu.VMEM((2, 4, D), F32),
            pltpu.VMEM((4, D), F32),
            pltpu.VMEM((4, D), F32),
            pltpu.VMEM((4, D), F32),
            pltpu.VMEM((2, D, T), BF16),
            pltpu.VMEM((2, T, D), BF16),
            pltpu.VMEM((D, D), BF16),
            pltpu.VMEM((D, D), BF16),
            pltpu.VMEM((RING, 64, D), BF16),
            pltpu.VMEM((RING, 64, D), BF16),
            pltpu.VMEM((64, D), F32),
            pltpu.VMEM((64, D), BF16),
            pltpu.VMEM((RING, 64, D), BF16),
            pltpu.VMEM((2, D, D), BF16),
            pltpu.VMEM((T, D), BF16),
            dma((9,)),
            dma((4,)), dma((4,)),
            dma((RING, PARTS)), dma((RING, PARTS)),
            dma((RING, PARTS)), dma((RING, PARTS)),
            dma((RING, PARTS)), dma((RING, PARTS)),
            dma((RING, PARTS)), dma((RING, PARTS)),
            dma((2,)), dma((2,)),
        ],
        compiler_params=pltpu.CompilerParams(
            collective_id=0, has_side_effects=True, vmem_limit_bytes=63_000_000
        ),
        cost_estimate=pl.CostEstimate(
            flops=16 * T * D * D, bytes_accessed=3 * 1024 * 1024, transcendentals=2 * T * D
        ),
        name="update_and_apply",
    )(*args)
    return pl.pallas_call(
        store_kernel,
        out_shape=shapes,
        in_specs=[hbm] * 3,
        out_specs=(hbm, hbm, hbm),
        scratch_shapes=[dma((3,))],
        compiler_params=pltpu.CompilerParams(vmem_limit_bytes=1024 * 1024),
        name="store",
    )(*results)


def solution(mesh):
    tokens = P("head", "ctx", None)
    weight = P("head", None, None)
    return jax.shard_map(
        per_device,
        mesh=mesh,
        in_specs=(tokens, tokens, tokens, P("head", "ctx"), weight, weight, weight, tokens, tokens),
        out_specs=(tokens, tokens, tokens),
        check_vma=False,
    )
```
